32 devices in a mesh: wide: 16 (over z, x, core), narrow: 2 (over y).
Axes of the slice: x: 2, y: 2, z: 4, core: 2. Of those that a mesh axis runs over, the one named last changes fastest.
Arguments:
- tensor: bfloat16 [16, 4096, 2048], P(None, 'wide', 'narrow'), may hold values from -100 to 100
- first_factor: bfloat16 [16, 256], replicated, may hold values from -8 to 8
- third_factor: bfloat16 [2048, 256], P('narrow'), may hold values from -10 to 10
Outputs:
- second_factor: bfloat16 [4096, 256], P('wide')
- third_new: bfloat16 [2048, 256], P('narrow')
- first_mode: float32 [16, 256], replicated
The draws below stay inside these ranges and needn't reach their ends.
All inputs are finite; a program needn't handle non-finite values.
Results may differ from the reference program's by a relative error of at most 0.008.
Values may be sent and summed in bfloat16 or wider, within the bound.
A program may use at most 128 MiB of HBM per device.

```python
import math
import jax
import jax.numpy as jnp
from jax import lax

I = 16
R = 256
J = 4096
K = 2048


def draw_tensor(key, part):
    keys = jax.random.split(jax.random.fold_in(key, 11), 4)
    noise = jnp.clip(jax.random.normal(keys[0], (I, J, K), jnp.float32), -4.0, 4.0)
    ramp_second = jnp.exp(math.log(3.0) * jnp.arange(J, dtype=jnp.float32) / J + jax.random.uniform(keys[1], (J,), jnp.float32, -0.7, 0.7)) / 1.5
    ramp_third = jnp.exp(math.log(3.0) * jnp.arange(K, dtype=jnp.float32) / K + jax.random.uniform(keys[2], (K,), jnp.float32, -0.7, 0.7)) / 1.5
    scale_first = jax.random.uniform(keys[3], (I,), jnp.float32, 0.7, 1.4)
    values = noise * scale_first[:, None, None] * ramp_second[None, :, None] * ramp_third[None, None, :]
    return values.astype(jnp.bfloat16)


def draw_first_factor(key, part):
    keys = jax.random.split(jax.random.fold_in(key, 37), 4)
    signs = jnp.where(jax.random.randint(keys[0], (I,), 0, 2) == 0, -1.0, 1.0).astype(jnp.float32)
    sizes_first = jax.random.uniform(keys[1], (I,), jnp.float32, 2.0, 3.0) * signs
    shared = jnp.exp(jax.random.uniform(keys[2], (R,), jnp.float32, math.log(0.6), math.log(1.8)))
    noise = jnp.clip(jax.random.normal(keys[3], (I, R), jnp.float32), -3.0, 3.0)
    values = sizes_first[:, None] * shared[None, :] + 0.3 * noise
    return jnp.clip(values, -8.0, 8.0).astype(jnp.bfloat16)


def draw_third_factor(key, part):
    keys = jax.random.split(jax.random.fold_in(key, 23), 3)
    common = jnp.clip(jax.random.normal(keys[1], (K,), jnp.float32), -3.0, 3.0)
    powers = 30.0 * jnp.exp(math.log(0.0001) * jnp.arange(R, dtype=jnp.float32) / (R - 1))
    mixing = jax.random.normal(keys[2], (R, R), jnp.float32) / math.sqrt(R) * jnp.sqrt(powers)[:, None]
    base = jnp.clip(jax.random.normal(keys[0], (K, R), jnp.float32), -4.0, 4.0)
    values = jnp.dot(base, mixing, precision=lax.Precision.HIGHEST) + common[:, None]
    return jnp.clip(values, -10.0, 10.0).astype(jnp.bfloat16)


def setup_inputs(seed: int = 0) -> dict:
    splits = jax.random.split(jax.random.key(seed), 4)
    return {
        "tensor": draw_tensor(jax.random.fold_in(splits[3], 71), 0),
        "first_factor": draw_first_factor(jax.random.fold_in(splits[3], 71), 0),
        "third_factor": draw_third_factor(jax.random.fold_in(splits[3], 71), 0),
    }


ridge = 0.5

def solve_rows(rows, system):
    lower = jnp.linalg.cholesky(system)
    return jax.scipy.linalg.cho_solve((lower, True), rows.T).T

def reference(tensor, first_factor, third_factor):
    first_wide = first_factor.astype(jnp.float32)
    gram_first = jnp.dot(first_factor.T.astype(jnp.float32), first_factor.astype(jnp.float32), preferred_element_type=jnp.float32) / I
    gram_third = jnp.dot(third_factor.T.astype(jnp.float32), third_factor.astype(jnp.float32), preferred_element_type=jnp.float32) / K
    identity = jnp.eye(R, dtype=jnp.float32)
    system_second = gram_first * gram_third + ridge * identity

    def accumulate(total, pieces):
        slab, coeffs = pieces
        return (total + coeffs[None, :] * jnp.dot(slab.astype(jnp.float32), third_factor.astype(jnp.float32), preferred_element_type=jnp.float32), None)
    mttkrp_second, unused = lax.scan(accumulate, jnp.zeros((J, R), jnp.float32), (tensor, first_wide))
    mttkrp_second = mttkrp_second / math.sqrt(I * K)
    second_factor = solve_rows(mttkrp_second, system_second).astype(jnp.bfloat16)
    gram_second = jnp.dot(second_factor.T.astype(jnp.float32), second_factor.astype(jnp.float32), preferred_element_type=jnp.float32) / J
    system_third = gram_first * gram_second + ridge * identity
    middle = lax.map(lambda slab: jnp.dot(slab.T.astype(jnp.float32), second_factor.astype(jnp.float32), preferred_element_type=jnp.float32), tensor)
    mttkrp_third = jnp.einsum('ikr,ir->kr', middle, first_wide, precision=lax.Precision.HIGHEST) / math.sqrt(I * J)
    third_solution = solve_rows(mttkrp_third, system_third)
    third_new = third_solution.astype(jnp.bfloat16)
    first_mode = jnp.einsum('ikr,kr->ir', middle, third_solution, precision=lax.Precision.HIGHEST) / math.sqrt(J * K)
    return (second_factor, third_new, first_mode)
```

```python
import functools
import math

import jax
import jax.numpy as jnp
from jax import lax
from jax.experimental import pallas as pl
from jax.experimental.pallas import tpu as pltpu
from jax.sharding import PartitionSpec as P

ridge = 0.5
F32 = jnp.float32
BF16 = jnp.bfloat16
HIGH = lax.Precision.HIGHEST
VM = pl.BlockSpec(memory_space=pltpu.VMEM)
MESH = pl.DeviceIdType.MESH


def params(**more):
    return pltpu.CompilerParams(vmem_limit_bytes=50 * 2**20, **more)


def remote(src, dst, sems, slot, wide, narrow):
    copy = pltpu.make_async_remote_copy(
        src_ref=src, dst_ref=dst, send_sem=sems.at[0, slot], recv_sem=sems.at[1, slot],
        device_id=(wide, narrow), device_id_type=MESH,
    )
    copy.start()
    return copy


def greet(partners):
    barrier = pltpu.get_barrier_semaphore()
    for partner in partners:
        pl.semaphore_signal(barrier, inc=1, device_id=partner, device_id_type=MESH)
    pl.semaphore_wait(barrier, len(partners))


def wait_all(copies):
    for copy in copies:
        copy.wait()


def second_kernel(t_ref, u_ref, w_ref, out_ref):
    step = pl.program_id(0)
    rank = w_ref.shape[1]

    @pl.when(step == 0)
    def _():
        out_ref[pl.ds(0, rank), :] = lax.dot_general(
            w_ref[...], w_ref[...], (((0,), (0,)), ((), ())), preferred_element_type=F32
        )
        out_ref[pl.ds(rank, t_ref.shape[1]), :] = jnp.zeros((t_ref.shape[1], rank), F32)

    out_ref[pl.ds(rank, t_ref.shape[1]), :] += u_ref[0] * jnp.dot(
        t_ref[0], w_ref[...], preferred_element_type=F32
    )


def second_products(tensor, first_wide, third):
    window, rows, depth = tensor.shape
    rank = third.shape[1]
    return pl.pallas_call(
        second_kernel,
        grid=(window,),
        in_specs=[
            pl.BlockSpec((1, rows, depth), lambda i: (i, 0, 0)),
            pl.BlockSpec((1, 1, rank), lambda i: (i, 0, 0)),
            pl.BlockSpec((depth, rank), lambda i: (0, 0)),
        ],
        out_specs=pl.BlockSpec((rank + rows, rank), lambda i: (0, 0)),
        out_shape=jax.ShapeDtypeStruct((rank + rows, rank), F32),
        compiler_params=params(),
    )(tensor, first_wide, third)


def narrow_kernel(count, x_ref, out_ref, land, sems):
    wide, narrow = lax.axis_index("wide"), lax.axis_index("narrow")
    others = [lax.rem(narrow + d, count) for d in range(1, count)]
    greet([(wide, other) for other in others])
    wait_all([remote(x_ref, land.at[d], sems, d, wide, other) for d, other in enumerate(others)])
    out_ref[...] = x_ref[...]
    for d in range(count - 1):
        out_ref[...] += land[d]


def narrow_sum(x, count):
    return pl.pallas_call(
        functools.partial(narrow_kernel, count),
        in_specs=[VM],
        out_specs=VM,
        out_shape=jax.ShapeDtypeStruct(x.shape, F32),
        scratch_shapes=[
            pltpu.VMEM((count - 1,) + x.shape, F32),
            pltpu.SemaphoreType.DMA((2, count - 1)),
        ],
        compiler_params=params(collective_id=0, has_side_effects=True),
    )(x)


def third_kernel(t_ref, u_ref, v_ref, mid_ref, out_ref):
    step = pl.program_id(0)
    part = lax.dot_general(
        t_ref[0], v_ref[...], (((0,), (0,)), ((), ())), preferred_element_type=F32
    )
    mid_ref[0] = part

    @pl.when(step == 0)
    def _():
        out_ref[...] = u_ref[0] * part

    @pl.when(step > 0)
    def _():
        out_ref[...] += u_ref[0] * part


def third_products(tensor, first_wide, second):
    window, rows, depth = tensor.shape
    rank = second.shape[1]
    return pl.pallas_call(
        third_kernel,
        grid=(window,),
        in_specs=[
            pl.BlockSpec((1, rows, depth), lambda i: (i, 0, 0)),
            pl.BlockSpec((1, 1, rank), lambda i: (i, 0, 0)),
            pl.BlockSpec((rows, rank), lambda i: (0, 0)),
        ],
        out_specs=[
            pl.BlockSpec((1, depth, rank), lambda i: (i, 0, 0)),
            pl.BlockSpec((depth, rank), lambda i: (0, 0)),
        ],
        out_shape=[
            jax.ShapeDtypeStruct((window, depth, rank), F32),
            jax.ShapeDtypeStruct((depth, rank), F32),
        ],
        compiler_params=params(),
    )(tensor, first_wide, second)


def place(size):
    wide, narrow = lax.axis_index("wide"), lax.axis_index("narrow")
    chips = size // 2
    chip, core = wide // 2, lax.rem(wide, 2)
    peer = chip * 2 + 1 - core
    others = [lax.rem(chip + d, chips) for d in range(1, chips)]
    return wide, narrow, chips, chip, core, peer, others


def wide_kernel(size, gram_ref, prod_ref, gram_out, prod_out,
                gram_land, prod_land, gram_acc, prod_acc, gram_parts, prod_parts,
                core_sems, gram_sems, prod_sems, share_sems):
    wide, narrow, chips, chip, core, peer, others = place(size)
    greet([(peer, narrow)] + [(other * 2 + core, narrow) for other in others])
    g_half, p_half = gram_ref.shape[0] // 2, prod_ref.shape[0] // 2
    g_rows, p_rows = g_half // chips, p_half // chips

    def part(ref, index, rows):
        return ref.at[pl.ds(pl.multiple_of(index * rows, rows), rows)]

    first = remote(part(gram_ref, 1 - core, g_half), gram_land, core_sems, 0, peer, narrow)
    next_ = remote(part(prod_ref, 1 - core, p_half), prod_land, core_sems, 1, peer, narrow)
    first.wait()
    gram_acc[...] = part(gram_ref, core, g_half)[...] + gram_land[...]
    grams = [remote(part(gram_acc, other, g_rows), gram_parts.at[d], gram_sems, d,
                    other * 2 + core, narrow) for d, other in enumerate(others)]
    next_.wait()
    prod_acc[...] = part(prod_ref, core, p_half)[...] + prod_land[...]
    wait_all(grams)
    total = part(gram_acc, chip, g_rows)[...]
    for d in range(chips - 1):
        total += gram_parts[d]
    mine = part(gram_out, core * chips + chip, g_rows)
    mine[...] = total
    shares = [remote(mine, mine, share_sems, d, other * 2 + core, narrow)
              for d, other in enumerate(others)]
    prods = [remote(part(prod_acc, other, p_rows), prod_parts.at[d], prod_sems, d,
                    other * 2 + core, narrow) for d, other in enumerate(others)]
    wait_all(shares)
    half = part(gram_out, core, g_half)
    last = remote(half, half, core_sems, 2, peer, narrow)
    wait_all(prods)
    total = part(prod_acc, chip, p_rows)[...]
    for d in range(chips - 1):
        total += prod_parts[d]
    prod_out[...] = total
    last.wait()


def wide_sums(gram, prod, size):
    rank = gram.shape[1]
    chips = size // 2
    g_half, p_half = gram.shape[0] // 2, prod.shape[0] // 2
    g_rows, p_rows = g_half // chips, p_half // chips
    return pl.pallas_call(
        functools.partial(wide_kernel, size),
        in_specs=[VM, VM],
        out_specs=[VM, VM],
        out_shape=[
            jax.ShapeDtypeStruct(gram.shape, F32),
            jax.ShapeDtypeStruct((p_rows, rank), F32),
        ],
        scratch_shapes=[
            pltpu.VMEM((g_half, rank), F32),
            pltpu.VMEM((p_half, rank), F32),
            pltpu.VMEM((g_half, rank), F32),
            pltpu.VMEM((p_half, rank), F32),
            pltpu.VMEM((chips - 1, g_rows, rank), F32),
            pltpu.VMEM((chips - 1, p_rows, rank), F32),
            pltpu.SemaphoreType.DMA((2, 3)),
            pltpu.SemaphoreType.DMA((2, chips - 1)),
            pltpu.SemaphoreType.DMA((2, chips - 1)),
            pltpu.SemaphoreType.DMA((2, chips - 1)),
        ],
        compiler_params=params(collective_id=1, has_side_effects=True),
    )(gram, prod)


def gather_kernel(size, x_ref, out_ref, sems, core_sems):
    wide, narrow, chips, chip, core, peer, others = place(size)
    greet([(peer, narrow)] + [(other * 2 + core, narrow) for other in others])
    rows = x_ref.shape[0]
    half = rows * chips
    mine = out_ref.at[pl.ds(pl.multiple_of((core * chips + chip) * rows, rows), rows)]
    copies = [remote(x_ref, mine, sems, d, other * 2 + core, narrow)
              for d, other in enumerate(others)]
    mine[...] = x_ref[...]
    wait_all(copies)
    side = out_ref.at[pl.ds(pl.multiple_of(core * half, half), half)]
    remote(side, side, core_sems, 0, peer, narrow).wait()


def gather_rows(x, size):
    return pl.pallas_call(
        functools.partial(gather_kernel, size),
        in_specs=[VM],
        out_specs=VM,
        out_shape=jax.ShapeDtypeStruct((x.shape[0] * size, x.shape[1]), x.dtype),
        scratch_shapes=[
            pltpu.SemaphoreType.DMA((2, size // 2 - 1)),
            pltpu.SemaphoreType.DMA((2, 1)),
        ],
        compiler_params=params(collective_id=2, has_side_effects=True),
    )(x)


def first_kernel(mid_ref, z_ref, out_ref):
    out_ref[0] = jnp.sum(mid_ref[0] * z_ref[...].astype(F32), axis=0, keepdims=True)


def first_products(middle, third_new):
    window, depth, rank = middle.shape
    return pl.pallas_call(
        first_kernel,
        grid=(window,),
        in_specs=[
            pl.BlockSpec((1, depth, rank), lambda i: (i, 0, 0)),
            pl.BlockSpec((depth, rank), lambda i: (0, 0)),
        ],
        out_specs=pl.BlockSpec((1, 1, rank), lambda i: (i, 0, 0)),
        out_shape=jax.ShapeDtypeStruct((window, 1, rank), F32),
        compiler_params=params(),
    )(middle, third_new)


def total_kernel(size, count, x_ref, out_ref, land, acc, parts, core_sems, sems):
    wide, narrow, chips, chip, core, peer, others = place(size)
    partners = []
    for d in range(chips):
        for e in range(count):
            if d or e:
                partners.append((lax.rem(chip + d, chips) * 2 + core, lax.rem(narrow + e, count)))
    greet([(peer, narrow)] + partners)
    half = x_ref.shape[0] // 2
    theirs = x_ref.at[pl.ds(pl.multiple_of((1 - core) * half, half), half)]
    mine = pl.ds(pl.multiple_of(core * half, half), half)
    remote(theirs, land, core_sems, 0, peer, narrow).wait()
    acc[...] = x_ref[mine, :] + land[...]
    wait_all([remote(acc, parts.at[d], sems, d, *partner) for d, partner in enumerate(partners)])
    total = acc[...]
    for d in range(len(partners)):
        total += parts[d]
    out_ref[mine, :] = total
    remote(out_ref.at[mine], out_ref.at[mine], core_sems, 1, peer, narrow).wait()


def total_sum(x, size, count):
    partners = size // 2 * count - 1
    half = (x.shape[0] // 2, x.shape[1])
    return pl.pallas_call(
        functools.partial(total_kernel, size, count),
        in_specs=[VM],
        out_specs=VM,
        out_shape=jax.ShapeDtypeStruct(x.shape, F32),
        scratch_shapes=[
            pltpu.VMEM(half, F32),
            pltpu.VMEM(half, F32),
            pltpu.VMEM((partners,) + half, F32),
            pltpu.SemaphoreType.DMA((2, 2)),
            pltpu.SemaphoreType.DMA((2, partners)),
        ],
        compiler_params=params(collective_id=3, has_side_effects=True),
    )(x)


def solve_rows(rows, system):
    lower = jnp.linalg.cholesky(system)
    return jax.scipy.linalg.cho_solve((lower, True), rows.T).T


def on_device(size, count, tensor, first_factor, third_factor):
    window, second_local, third_local = tensor.shape
    rank = first_factor.shape[1]
    second_total = second_local * size
    third_total = third_local * count
    first_wide = first_factor.astype(F32).reshape(window, 1, rank)
    identity = jnp.eye(rank, dtype=F32)
    gram_first = jnp.dot(first_factor.T, first_factor, preferred_element_type=F32) / window
    sums = narrow_sum(second_products(tensor, first_wide, third_factor), count)
    gram_third = sums[:rank] / third_total
    mttkrp_second = sums[rank:] / math.sqrt(window * third_total)
    system_second = gram_first * gram_third + ridge * identity
    second_factor = solve_rows(mttkrp_second, system_second).astype(BF16)
    gram_local = jnp.dot(second_factor.T, second_factor, preferred_element_type=F32)
    middle, partial_third = third_products(tensor, first_wide, second_factor)
    gram_second, rows_third = wide_sums(gram_local, partial_third, size)
    system_third = gram_first * (gram_second / second_total) + ridge * identity
    mttkrp_third = rows_third / math.sqrt(window * second_total)
    third_rows = solve_rows(mttkrp_third, system_third).astype(BF16)
    third_new = gather_rows(third_rows, size)
    partial_first = first_products(middle, third_new).reshape(window, rank)
    first_mode = total_sum(partial_first, size, count) / math.sqrt(second_total * third_total)
    return (second_factor, third_new, first_mode)


def solution(mesh):
    size, count = mesh.shape["wide"], mesh.shape["narrow"]
    in_specs = (P(None, "wide", "narrow"), P(), P("narrow", None))
    out_specs = (P("wide", None), P("narrow", None), P())
    return jax.shard_map(
        functools.partial(on_device, size, count), mesh=mesh,
        in_specs=in_specs, out_specs=out_specs, check_vma=False,
    )
```

```python
import functools
import math

import jax
import jax.numpy as jnp
from jax import lax
from jax.experimental import pallas as pl
from jax.experimental.pallas import tpu as pltpu
from jax.sharding import PartitionSpec as P

ridge = 0.5
F32 = jnp.float32
BF16 = jnp.bfloat16
HIGH = lax.Precision.HIGHEST
VM = pl.BlockSpec(memory_space=pltpu.VMEM)
MESH = pl.DeviceIdType.MESH


def params(**more):
    return pltpu.CompilerParams(vmem_limit_bytes=50 * 2**20, **more)


def remote(src, dst, sems, slot, wide, narrow):
    copy = pltpu.make_async_remote_copy(
        src_ref=src, dst_ref=dst, send_sem=sems.at[0, slot], recv_sem=sems.at[1, slot],
        device_id=(wide, narrow), device_id_type=MESH,
    )
    copy.start()
    return copy


def greet(partners):
    barrier = pltpu.get_barrier_semaphore()
    for partner in partners:
        pl.semaphore_signal(barrier, inc=1, device_id=partner, device_id_type=MESH)
    pl.semaphore_wait(barrier, len(partners))


def wait_all(copies):
    for copy in copies:
        copy.wait()


def second_kernel(t_ref, u_ref, w_ref, out_ref):
    step = pl.program_id(0)
    rank = w_ref.shape[1]
    slabs, rows, depth = t_ref.shape
    here = pl.ds(rank, rows)

    @pl.when(step == 0)
    def _():
        out_ref[pl.ds(0, rank), :] = lax.dot_general(
            w_ref[...], w_ref[...], (((0,), (0,)), ((), ())), preferred_element_type=F32
        )
        out_ref[here, :] = jnp.zeros((rows, rank), F32)

    product = jnp.dot(
        t_ref[...].reshape(slabs * rows, depth), w_ref[...], preferred_element_type=F32
    ).reshape(slabs, rows, rank)
    total = out_ref[here, :]
    for s in range(slabs):
        total += u_ref[s] * product[s]
    out_ref[here, :] = total


def second_products(tensor, first_wide, third):
    window, rows, depth = tensor.shape
    rank = third.shape[1]
    slabs = math.gcd(window, 4)
    return pl.pallas_call(
        second_kernel,
        grid=(window // slabs,),
        in_specs=[
            pl.BlockSpec((slabs, rows, depth), lambda i: (i, 0, 0)),
            pl.BlockSpec((slabs, 1, rank), lambda i: (i, 0, 0)),
            pl.BlockSpec((depth, rank), lambda i: (0, 0)),
        ],
        out_specs=pl.BlockSpec((rank + rows, rank), lambda i: (0, 0)),
        out_shape=jax.ShapeDtypeStruct((rank + rows, rank), F32),
        compiler_params=params(),
    )(tensor, first_wide, third)


def narrow_kernel(count, x_ref, out_ref, land, sems):
    wide, narrow = lax.axis_index("wide"), lax.axis_index("narrow")
    others = [lax.rem(narrow + d, count) for d in range(1, count)]
    greet([(wide, other) for other in others])
    wait_all([remote(x_ref, land.at[d], sems, d, wide, other) for d, other in enumerate(others)])
    out_ref[...] = x_ref[...]
    for d in range(count - 1):
        out_ref[...] += land[d]


def narrow_sum(x, count):
    return pl.pallas_call(
        functools.partial(narrow_kernel, count),
        in_specs=[VM],
        out_specs=VM,
        out_shape=jax.ShapeDtypeStruct(x.shape, F32),
        scratch_shapes=[
            pltpu.VMEM((count - 1,) + x.shape, F32),
            pltpu.SemaphoreType.DMA((2, count - 1)),
        ],
        compiler_params=params(collective_id=0, has_side_effects=True),
    )(x)


def third_kernel(t_ref, u_ref, v_ref, mid_ref, out_ref, acc):
    step = pl.program_id(0)

    @pl.when(step == 0)
    def _():
        acc[...] = jnp.zeros(acc.shape, F32)

    turned = v_ref[...]
    for s in range(t_ref.shape[0]):
        part = jnp.dot(turned, t_ref[s], preferred_element_type=F32)
        mid_ref[s] = part.astype(BF16)
        acc[...] += u_ref[s] * part

    @pl.when(step == pl.num_programs(0) - 1)
    def _():
        out_ref[...] = acc[...].T


def third_products(tensor, first_tall, second_turned):
    window, rows, depth = tensor.shape
    rank = second_turned.shape[0]
    slabs = math.gcd(window, 2)
    return pl.pallas_call(
        third_kernel,
        grid=(window // slabs,),
        in_specs=[
            pl.BlockSpec((slabs, rows, depth), lambda i: (i, 0, 0)),
            pl.BlockSpec((slabs, rank, 1), lambda i: (i, 0, 0)),
            pl.BlockSpec((rank, rows), lambda i: (0, 0)),
        ],
        out_specs=[
            pl.BlockSpec((slabs, rank, depth), lambda i: (i, 0, 0)),
            pl.BlockSpec((depth, rank), lambda i: (0, 0)),
        ],
        out_shape=[
            jax.ShapeDtypeStruct((window, rank, depth), BF16),
            jax.ShapeDtypeStruct((depth, rank), F32),
        ],
        scratch_shapes=[pltpu.VMEM((rank, depth), F32)],
        compiler_params=params(),
    )(tensor, first_tall, second_turned)


def place(size):
    wide, narrow = lax.axis_index("wide"), lax.axis_index("narrow")
    chips = size // 2
    chip, core = wide // 2, lax.rem(wide, 2)
    peer = chip * 2 + 1 - core
    others = [lax.rem(chip + d, chips) for d in range(1, chips)]
    return wide, narrow, chips, chip, core, peer, others


def wide_kernel(size, gram_ref, prod_ref, gram_out, prod_out,
                gram_land, prod_land, gram_acc, prod_acc, gram_parts, prod_parts,
                core_sems, gram_sems, prod_sems, share_sems):
    wide, narrow, chips, chip, core, peer, others = place(size)
    greet([(peer, narrow)] + [(other * 2 + core, narrow) for other in others])
    g_half, p_half = gram_ref.shape[0] // 2, prod_ref.shape[0] // 2
    g_rows, p_rows = g_half // chips, p_half // chips

    def part(ref, index, rows):
        return ref.at[pl.ds(pl.multiple_of(index * rows, rows), rows)]

    first = remote(part(gram_ref, 1 - core, g_half), gram_land, core_sems, 0, peer, narrow)
    next_ = remote(part(prod_ref, 1 - core, p_half), prod_land, core_sems, 1, peer, narrow)
    first.wait()
    gram_acc[...] = part(gram_ref, core, g_half)[...] + gram_land[...]
    grams = [remote(part(gram_acc, other, g_rows), gram_parts.at[d], gram_sems, d,
                    other * 2 + core, narrow) for d, other in enumerate(others)]
    next_.wait()
    prod_acc[...] = part(prod_ref, core, p_half)[...] + prod_land[...]
    wait_all(grams)
    total = part(gram_acc, chip, g_rows)[...]
    for d in range(chips - 1):
        total += gram_parts[d]
    mine = part(gram_out, core * chips + chip, g_rows)
    mine[...] = total
    shares = [remote(mine, mine, share_sems, d, other * 2 + core, narrow)
              for d, other in enumerate(others)]
    prods = [remote(part(prod_acc, other, p_rows), prod_parts.at[d], prod_sems, d,
                    other * 2 + core, narrow) for d, other in enumerate(others)]
    wait_all(shares)
    half = part(gram_out, core, g_half)
    last = remote(half, half, core_sems, 2, peer, narrow)
    wait_all(prods)
    total = part(prod_acc, chip, p_rows)[...]
    for d in range(chips - 1):
        total += prod_parts[d]
    prod_out[...] = total
    last.wait()


def wide_sums(gram, prod, size):
    rank = gram.shape[1]
    chips = size // 2
    g_half, p_half = gram.shape[0] // 2, prod.shape[0] // 2
    g_rows, p_rows = g_half // chips, p_half // chips
    return pl.pallas_call(
        functools.partial(wide_kernel, size),
        in_specs=[VM, VM],
        out_specs=[VM, VM],
        out_shape=[
            jax.ShapeDtypeStruct(gram.shape, F32),
            jax.ShapeDtypeStruct((p_rows, rank), F32),
        ],
        scratch_shapes=[
            pltpu.VMEM((g_half, rank), F32),
            pltpu.VMEM((p_half, rank), F32),
            pltpu.VMEM((g_half, rank), F32),
            pltpu.VMEM((p_half, rank), F32),
            pltpu.VMEM((chips - 1, g_rows, rank), F32),
            pltpu.VMEM((chips - 1, p_rows, rank), F32),
            pltpu.SemaphoreType.DMA((2, 3)),
            pltpu.SemaphoreType.DMA((2, chips - 1)),
            pltpu.SemaphoreType.DMA((2, chips - 1)),
            pltpu.SemaphoreType.DMA((2, chips - 1)),
        ],
        compiler_params=params(collective_id=1, has_side_effects=True),
    )(gram, prod)


def gather_kernel(size, x_ref, out_ref, sems, core_sems):
    wide, narrow, chips, chip, core, peer, others = place(size)
    greet([(peer, narrow)] + [(other * 2 + core, narrow) for other in others])
    rows = x_ref.shape[0]
    half = rows * chips
    mine = out_ref.at[pl.ds(pl.multiple_of((core * chips + chip) * rows, rows), rows)]
    copies = [remote(x_ref, mine, sems, d, other * 2 + core, narrow)
              for d, other in enumerate(others)]
    mine[...] = x_ref[...]
    wait_all(copies)
    side = out_ref.at[pl.ds(pl.multiple_of(core * half, half), half)]
    remote(side, side, core_sems, 0, peer, narrow).wait()


def gather_rows(x, size):
    return pl.pallas_call(
        functools.partial(gather_kernel, size),
        in_specs=[VM],
        out_specs=VM,
        out_shape=jax.ShapeDtypeStruct((x.shape[0] * size, x.shape[1]), x.dtype),
        scratch_shapes=[
            pltpu.SemaphoreType.DMA((2, size // 2 - 1)),
            pltpu.SemaphoreType.DMA((2, 1)),
        ],
        compiler_params=params(collective_id=2, has_side_effects=True),
    )(x)


def first_kernel(mid_ref, z_ref, out_ref):
    turned = z_ref[...].astype(F32).T
    sums = [
        jnp.sum(mid_ref[s].astype(F32) * turned, axis=1, keepdims=True)
        for s in range(mid_ref.shape[0])
    ]
    out_ref[0] = jnp.concatenate(sums, axis=1).T


def first_products(middle, third_new):
    window, rank, depth = middle.shape
    slabs = math.gcd(window, 4)
    return pl.pallas_call(
        first_kernel,
        grid=(window // slabs,),
        in_specs=[
            pl.BlockSpec((slabs, rank, depth), lambda i: (i, 0, 0)),
            pl.BlockSpec((depth, rank), lambda i: (0, 0)),
        ],
        out_specs=pl.BlockSpec((1, slabs, rank), lambda i: (i, 0, 0)),
        out_shape=jax.ShapeDtypeStruct((window // slabs, slabs, rank), F32),
        compiler_params=params(),
    )(middle, third_new)


def total_kernel(size, count, x_ref, out_ref, land, acc, parts, core_sems, sems):
    wide, narrow, chips, chip, core, peer, others = place(size)
    partners = []
    for d in range(chips):
        for e in range(count):
            if d or e:
                partners.append((lax.rem(chip + d, chips) * 2 + core, lax.rem(narrow + e, count)))
    greet([(peer, narrow)] + partners)
    half = x_ref.shape[0] // 2
    theirs = x_ref.at[pl.ds(pl.multiple_of((1 - core) * half, half), half)]
    mine = pl.ds(pl.multiple_of(core * half, half), half)
    remote(theirs, land, core_sems, 0, peer, narrow).wait()
    acc[...] = x_ref[mine, :] + land[...]
    wait_all([remote(acc, parts.at[d], sems, d, *partner) for d, partner in enumerate(partners)])
    total = acc[...]
    for d in range(len(partners)):
        total += parts[d]
    out_ref[mine, :] = total
    remote(out_ref.at[mine], out_ref.at[mine], core_sems, 1, peer, narrow).wait()


def total_sum(x, size, count):
    partners = size // 2 * count - 1
    half = (x.shape[0] // 2, x.shape[1])
    return pl.pallas_call(
        functools.partial(total_kernel, size, count),
        in_specs=[VM],
        out_specs=VM,
        out_shape=jax.ShapeDtypeStruct(x.shape, F32),
        scratch_shapes=[
            pltpu.VMEM(half, F32),
            pltpu.VMEM(half, F32),
            pltpu.VMEM((partners,) + half, F32),
            pltpu.SemaphoreType.DMA((2, 2)),
            pltpu.SemaphoreType.DMA((2, partners)),
        ],
        compiler_params=params(collective_id=3, has_side_effects=True),
    )(x)


GROUP = 8


def split(x):
    high = x.astype(BF16)
    rest = x - high.astype(F32)
    middle = rest.astype(BF16)
    return high, middle, (rest - middle.astype(F32)).astype(BF16)


def eliminate(rows, groups, at):
    shape = rows[0].shape
    width = 128
    lane = lax.broadcasted_iota(jnp.int32, shape, 1)
    sub = lax.broadcasted_iota(jnp.int32, shape, 0)
    narrow_sub = lax.broadcasted_iota(jnp.int32, (GROUP, width), 0)
    for a in range(groups):
        start = at + a * GROUP
        own = (lane >= start) & (lane < start + GROUP)
        columns = [
            jnp.broadcast_to(rows[a][:, start + j:start + j + 1], (GROUP, width)) for j in range(GROUP)
        ]
        target = jnp.where(own, jnp.where(lane - start == sub, 1.0, 0.0), rows[a])
        for j in range(GROUP):
            pivot = 1.0 / jnp.broadcast_to(columns[j][j:j + 1], (GROUP, width))
            factor = jnp.where(narrow_sub == j, -1.0, columns[j]) * pivot
            for l in range(j + 1, GROUP):
                row = jnp.broadcast_to(columns[l][j:j + 1], (GROUP, width))
                columns[l] = jnp.where(narrow_sub == j, 0.0, columns[l]) - factor * row
            wide = jnp.concatenate([factor] * (shape[1] // width), axis=1)
            row = jnp.broadcast_to(target[j:j + 1], shape)
            target = jnp.where(sub == j, 0.0, target) - wide * row
        for b in range(groups):
            if b != a:
                other = jnp.where(own, 0.0, rows[b])
                for j in range(GROUP):
                    other -= rows[b][:, start + j:start + j + 1] * target[j:j + 1]
                rows[b] = other
        rows[a] = target
    return rows


def invert(ref):
    size = ref.shape[0]
    panel = 32
    groups = panel // GROUP
    for at in range(0, size, panel):
        before = ref[pl.ds(at, panel), :]
        rows = eliminate(
            [before[g * GROUP:(g + 1) * GROUP] for g in range(groups)], groups, at
        )
        after = jnp.concatenate(rows, axis=0)
        lane = lax.broadcasted_iota(jnp.int32, before.shape, 1)
        h, m, l = split(jnp.where(lane < at, -before, before))
        left = jnp.concatenate([h, h, m, m, h, l], axis=0)
        h, m, l = split(after)
        right = jnp.concatenate([h, m, h, m, l, h], axis=0)
        update = lax.dot_general(
            left, right, (((0,), (0,)), ((), ())), preferred_element_type=F32
        )
        column = lax.broadcasted_iota(jnp.int32, (size, size), 1)
        inside = (column >= at) & (column < at + panel)
        ref[...] = jnp.where(inside, 0.0, ref[...]) - update
        ref[pl.ds(at, panel), :] = after


def solve_kernel(gram_scale, row_scale, ridge, u_ref, gram_ref, rows_ref, out_ref, local_ref, work):
    window = u_ref.shape[0]
    gram_first = lax.dot_general(
        u_ref[...], u_ref[...], (((0,), (0,)), ((), ())), preferred_element_type=F32
    ) * (1.0 / window)
    shape = work.shape
    diagonal = lax.broadcasted_iota(jnp.int32, shape, 0) == lax.broadcasted_iota(jnp.int32, shape, 1)
    system = gram_first * (gram_ref[...] * gram_scale)
    work[...] = jnp.where(diagonal, system + ridge, system)
    invert(work)
    out = jnp.dot(
        rows_ref[...] * row_scale, work[...], preferred_element_type=F32, precision=HIGH
    ).astype(BF16)
    out_ref[...] = out
    local_ref[...] = lax.dot_general(
        out, out, (((0,), (0,)), ((), ())), preferred_element_type=F32
    )

def solve(gram_scale, row_scale, first_factor, gram, rows):
    rank = gram.shape[0]
    return pl.pallas_call(
        functools.partial(solve_kernel, gram_scale, row_scale, ridge),
        in_specs=[VM] * 3,
        out_specs=[VM] * 2,
        out_shape=[
            jax.ShapeDtypeStruct(rows.shape, BF16),
            jax.ShapeDtypeStruct((rank, rank), F32),
        ],
        scratch_shapes=[pltpu.VMEM((rank, rank), F32)],
        compiler_params=params(),
    )(first_factor, gram, rows)


def on_device(size, count, tensor, first_factor, third_factor):
    window, second_local, third_local = tensor.shape
    rank = first_factor.shape[1]
    second_total = second_local * size
    third_total = third_local * count
    first_wide = first_factor.astype(F32).reshape(window, 1, rank)
    first_tall = first_factor.astype(F32).reshape(window, rank, 1)
    sums = narrow_sum(second_products(tensor, first_wide, third_factor), count)
    second_factor, gram_local = solve(
        1.0 / third_total, 1.0 / math.sqrt(window * third_total),
        first_factor, sums[:rank], sums[rank:],
    )
    middle, partial_third = third_products(tensor, first_tall, second_factor.T)
    gram_second, rows_third = wide_sums(gram_local, partial_third, size)
    third_rows, _ = solve(
        1.0 / second_total, 1.0 / math.sqrt(window * second_total),
        first_factor, gram_second, rows_third,
    )
    third_new = gather_rows(third_rows, size)
    partial_first = first_products(middle, third_new).reshape(window, rank)
    first_mode = total_sum(partial_first, size, count) / math.sqrt(second_total * third_total)
    return (second_factor, third_new, first_mode)


def solution(mesh):
    size, count = mesh.shape["wide"], mesh.shape["narrow"]
    in_specs = (P(None, "wide", "narrow"), P(), P("narrow", None))
    out_specs = (P("wide", None), P("narrow", None), P())
    return jax.shard_map(
        functools.partial(on_device, size, count), mesh=mesh,
        in_specs=in_specs, out_specs=out_specs, check_vma=False,
    )
```

```python
import functools
import math

import jax
import jax.numpy as jnp
from jax import lax
from jax.experimental import pallas as pl
from jax.experimental.pallas import tpu as pltpu
from jax.sharding import PartitionSpec as P

ridge = 0.5
F32 = jnp.float32
BF16 = jnp.bfloat16
HIGH = lax.Precision.HIGHEST
VM = pl.BlockSpec(memory_space=pltpu.VMEM)
MESH = pl.DeviceIdType.MESH


def params(**more):
    return pltpu.CompilerParams(vmem_limit_bytes=50 * 2**20, **more)


def remote(src, dst, sems, slot, wide, narrow):
    copy = pltpu.make_async_remote_copy(
        src_ref=src, dst_ref=dst, send_sem=sems.at[0, slot], recv_sem=sems.at[1, slot],
        device_id=(wide, narrow), device_id_type=MESH,
    )
    copy.start()
    return copy


def greet(partners):
    barrier = pltpu.get_barrier_semaphore()
    for partner in partners:
        pl.semaphore_signal(barrier, inc=1, device_id=partner, device_id_type=MESH)
    pl.semaphore_wait(barrier, len(partners))


def wait_all(copies):
    for copy in copies:
        copy.wait()


GROUP = 8


def split(x):
    high = x.astype(BF16)
    rest = x - high.astype(F32)
    middle = rest.astype(BF16)
    return high, middle, (rest - middle.astype(F32)).astype(BF16)


def eliminate(rows, groups, at):
    shape = rows[0].shape
    width = 128
    lane = lax.broadcasted_iota(jnp.int32, shape, 1)
    sub = lax.broadcasted_iota(jnp.int32, shape, 0)
    narrow_sub = lax.broadcasted_iota(jnp.int32, (GROUP, width), 0)
    for a in range(groups):
        start = at + a * GROUP
        own = (lane >= start) & (lane < start + GROUP)
        columns = [
            jnp.broadcast_to(rows[a][:, start + j:start + j + 1], (GROUP, width)) for j in range(GROUP)
        ]
        target = jnp.where(own, jnp.where(lane - start == sub, 1.0, 0.0), rows[a])
        for j in range(GROUP):
            pivot = 1.0 / jnp.broadcast_to(columns[j][j:j + 1], (GROUP, width))
            factor = jnp.where(narrow_sub == j, -1.0, columns[j]) * pivot
            for l in range(j + 1, GROUP):
                row = jnp.broadcast_to(columns[l][j:j + 1], (GROUP, width))
                columns[l] = jnp.where(narrow_sub == j, 0.0, columns[l]) - factor * row
            wide = jnp.concatenate([factor] * (shape[1] // width), axis=1)
            row = jnp.broadcast_to(target[j:j + 1], shape)
            target = jnp.where(sub == j, 0.0, target) - wide * row
        for b in range(groups):
            if b != a:
                other = jnp.where(own, 0.0, rows[b])
                for j in range(GROUP):
                    other -= rows[b][:, start + j:start + j + 1] * target[j:j + 1]
                rows[b] = other
        rows[a] = target
    return rows


def invert(ref):
    size = ref.shape[0]
    panel = 32
    groups = panel // GROUP

    def step(index, carry):
        at = pl.multiple_of(index * panel, panel)
        before = ref[pl.ds(at, panel), :]
        turned = pltpu.roll(before, size - at, 1)
        rows = eliminate(
            [turned[g * GROUP:(g + 1) * GROUP] for g in range(groups)], groups, 0
        )
        after = pltpu.roll(jnp.concatenate(rows, axis=0), at, 1)
        lane = lax.broadcasted_iota(jnp.int32, before.shape, 1)
        h, m, l = split(jnp.where(lane < at, -before, before))
        left = jnp.concatenate([h, h, m, m, h, l], axis=0)
        h, m, l = split(after)
        right = jnp.concatenate([h, m, h, m, l, h], axis=0)
        update = lax.dot_general(
            left, right, (((0,), (0,)), ((), ())), preferred_element_type=F32
        )
        column = lax.broadcasted_iota(jnp.int32, (size, size), 1)
        inside = (column >= at) & (column < at + panel)
        ref[...] = jnp.where(inside, 0.0, ref[...]) - update
        ref[pl.ds(at, panel), :] = after
        return carry

    lax.fori_loop(0, size // panel, step, 0)


def set_system(work, gram_first, gram):
    shape = work.shape
    diagonal = lax.broadcasted_iota(jnp.int32, shape, 0) == lax.broadcasted_iota(jnp.int32, shape, 1)
    system = gram_first * gram
    work[...] = jnp.where(diagonal, system + ridge, system)


PIECES = 4


def part(ref, index, rows):
    return ref.at[pl.ds(pl.multiple_of(index * rows, rows), rows)]


def sweep(size, count, t_hbm, u_ref, w_ref, second_out, third_out, first_out,
          t_ref, mid, acc, g_src, p_src, g_land, p_land, work,
          gl_src, gl_land, gl_acc, gl_parts, gl_all,
          prod_src, prod_land, prod_acc, prod_parts, z_src,
          f_src, f_land, f_acc, f_parts,
          load_sems, g_sems, p_sems, core_sems, gram_sems, share_sems, prod_sems,
          z_sems, z_core_sems, f_sems):
    wide, narrow = lax.axis_index("wide"), lax.axis_index("narrow")
    chips = size // 2
    chip, core = wide // 2, lax.rem(wide, 2)
    peer = chip * 2 + 1 - core
    others = [lax.rem(chip + d, chips) for d in range(1, chips)]
    across = [lax.rem(narrow + e, count) for e in range(1, count)]
    partners = []
    for d in range(chips):
        for e in range(count):
            if d or e:
                partners.append((lax.rem(chip + d, chips) * 2 + core, lax.rem(narrow + e, count)))

    window, rows, depth = t_ref.shape
    rank = u_ref.shape[1]
    slabs = window // PIECES
    second_total, third_total = rows * size, depth * count
    loads = [
        pltpu.make_async_copy(
            t_hbm.at[pl.ds(c * slabs, slabs)], t_ref.at[pl.ds(c * slabs, slabs)], load_sems.at[c]
        ) for c in range(PIECES)
    ]
    for load in loads:
        load.start()
    greet([(peer, narrow)] + partners)

    g_src[...] = lax.dot_general(
        w_ref[...], w_ref[...], (((0,), (0,)), ((), ())), preferred_element_type=F32
    )
    g_sends = [remote(g_src, g_land.at[d], g_sems, d, wide, e) for d, e in enumerate(across)]
    u_rows = u_ref[...].astype(F32)
    u_columns = u_rows.T
    gram_first = lax.dot_general(
        u_ref[...], u_ref[...], (((0,), (0,)), ((), ())), preferred_element_type=F32
    ) * (1.0 / window)
    for c in range(PIECES):
        loads[c].wait()
        product = jnp.dot(
            t_ref[pl.ds(c * slabs, slabs)].reshape(slabs * rows, depth), w_ref[...],
            preferred_element_type=F32,
        ).reshape(slabs, rows, rank)
        total = product[0] * u_rows[c * slabs:c * slabs + 1]
        for s in range(1, slabs):
            total += product[s] * u_rows[c * slabs + s:c * slabs + s + 1]
        p_src[...] = total if c == 0 else p_src[...] + total
    p_sends = [remote(p_src, p_land.at[d], p_sems, d, wide, e) for d, e in enumerate(across)]
    wait_all(g_sends)
    total = g_src[...]
    for d in range(count - 1):
        total += g_land[d]
    set_system(work, gram_first, total * (1.0 / third_total))
    invert(work)
    wait_all(p_sends)
    total = p_src[...]
    for d in range(count - 1):
        total += p_land[d]
    second = jnp.dot(
        total * (1.0 / math.sqrt(window * third_total)), work[...],
        preferred_element_type=F32, precision=HIGH,
    )
    second_out[...] = second.astype(BF16)
    turned = second.T.astype(BF16)
    gl_src[...] = jnp.dot(turned, second.astype(BF16), preferred_element_type=F32)

    g_half, p_half = rank // 2, depth // 2
    g_rows, p_rows = g_half // chips, p_half // chips

    def middle(first, last):
        for s in range(first, last):
            product = jnp.dot(turned, t_ref[s], preferred_element_type=F32)
            mid[s] = product.astype(BF16)
            scaled = product * u_columns[:, s:s + 1]
            acc[...] = scaled if s == 0 else acc[...] + scaled

    pair = remote(part(gl_src, 1 - core, g_half), gl_land, core_sems, 0, peer, narrow)
    middle(0, window // 4)
    pair.wait()
    gl_acc[...] = part(gl_src, core, g_half)[...] + gl_land[...]
    grams = [remote(part(gl_acc, other, g_rows), gl_parts.at[d], gram_sems, d,
                    other * 2 + core, narrow) for d, other in enumerate(others)]
    middle(window // 4, window * 5 // 8)
    wait_all(grams)
    total = part(gl_acc, chip, g_rows)[...]
    for d in range(chips - 1):
        total += gl_parts[d]
    mine = part(gl_all, core * chips + chip, g_rows)
    mine[...] = total
    shares = [remote(mine, mine, share_sems, d, other * 2 + core, narrow)
              for d, other in enumerate(others)]
    middle(window * 5 // 8, window)
    prod_src[...] = acc[...].T
    halves = remote(part(prod_src, 1 - core, p_half), prod_land, core_sems, 1, peer, narrow)
    wait_all(shares)
    half = part(gl_all, core, g_half)
    pair = remote(half, half, core_sems, 2, peer, narrow)
    halves.wait()
    prod_acc[...] = part(prod_src, core, p_half)[...] + prod_land[...]
    prods = [remote(part(prod_acc, other, p_rows), prod_parts.at[d], prod_sems, d,
                    other * 2 + core, narrow) for d, other in enumerate(others)]
    pair.wait()

    set_system(work, gram_first, gl_all[...] * (1.0 / second_total))
    invert(work)
    wait_all(prods)
    total = part(prod_acc, chip, p_rows)[...]
    for d in range(chips - 1):
        total += prod_parts[d]
    z_src[...] = jnp.dot(
        total * (1.0 / math.sqrt(window * second_total)), work[...],
        preferred_element_type=F32, precision=HIGH,
    ).astype(BF16)
    mine = part(third_out, core * chips + chip, p_rows)
    sends = [remote(z_src, mine, z_sems, d, other * 2 + core, narrow)
             for d, other in enumerate(others)]
    passes = [remote(z_src, mine, z_core_sems, 0, peer, narrow)]
    mine[...] = z_src[...]
    for d in range(1, chips):
        sends[d - 1].wait()
        block = part(third_out, core * chips + lax.rem(chip + chips - d, chips), p_rows)
        passes.append(remote(block, block, z_core_sems, d, peer, narrow))
    wait_all(passes)

    turned = third_out[...].astype(F32).T
    sums = [
        jnp.sum(mid[s].astype(F32) * turned, axis=1, keepdims=True) for s in range(window)
    ]
    f_src[...] = jnp.concatenate(sums, axis=1).T
    f_half = window // 2
    remote(part(f_src, 1 - core, f_half), f_land, core_sems, 3, peer, narrow).wait()
    f_acc[...] = part(f_src, core, f_half)[...] + f_land[...]
    wait_all([remote(f_acc, f_parts.at[d], f_sems, d, *partner)
              for d, partner in enumerate(partners)])
    total = f_acc[...]
    for d in range(len(partners)):
        total += f_parts[d]
    mine = part(first_out, core, f_half)
    mine[...] = total * (1.0 / math.sqrt(second_total * third_total))
    remote(mine, mine, core_sems, 4, peer, narrow).wait()


def on_device(size, count, tensor, first_factor, third_factor):
    window, rows, depth = tensor.shape
    rank = first_factor.shape[1]
    chips = size // 2
    partners = chips * count - 1
    g_rows, p_rows = rank // size, depth // size
    dma = pltpu.SemaphoreType.DMA

    def floats(*shape):
        return pltpu.VMEM(shape, F32)

    return pl.pallas_call(
        functools.partial(sweep, size, count),
        in_specs=[pl.BlockSpec(memory_space=pl.ANY), VM, VM],
        out_specs=[VM] * 3,
        out_shape=[
            jax.ShapeDtypeStruct((rows, rank), BF16),
            jax.ShapeDtypeStruct((depth, rank), BF16),
            jax.ShapeDtypeStruct((window, rank), F32),
        ],
        scratch_shapes=[
            pltpu.VMEM((window, rows, depth), BF16), pltpu.VMEM((window, rank, depth), BF16),
            floats(rank, depth), floats(rank, rank), floats(rows, rank),
            floats(count - 1, rank, rank), floats(count - 1, rows, rank), floats(rank, rank),
            floats(rank, rank), floats(rank // 2, rank), floats(rank // 2, rank),
            floats(chips - 1, g_rows, rank), floats(rank, rank),
            floats(depth, rank), floats(depth // 2, rank), floats(depth // 2, rank),
            floats(chips - 1, p_rows, rank), pltpu.VMEM((p_rows, rank), BF16),
            floats(window, rank), floats(window // 2, rank), floats(window // 2, rank),
            floats(partners, window // 2, rank),
            dma((PIECES,)), dma((2, count - 1)), dma((2, count - 1)), dma((2, 5)),
            dma((2, chips - 1)), dma((2, chips - 1)), dma((2, chips - 1)),
            dma((2, chips - 1)), dma((2, chips)), dma((2, partners)),
        ],
        compiler_params=params(collective_id=0, has_side_effects=True),
    )(tensor, first_factor, third_factor)


def solution(mesh):
    size, count = mesh.shape["wide"], mesh.shape["narrow"]
    in_specs = (P(None, "wide", "narrow"), P(), P("narrow", None))
    out_specs = (P("wide", None), P("narrow", None), P())
    return jax.shard_map(
        functools.partial(on_device, size, count), mesh=mesh,
        in_specs=in_specs, out_specs=out_specs, check_vma=False,
    )
```
